512 devices in a mesh: row: 16 (over x, y_hi, core), col: 32 (over z, y_lo).
Axes of the slice: x: 4, y: 4 (y_hi: 2, y_lo: 2; y = y_hi * 2 + y_lo), z: 16, core: 2. Of those that a mesh axis runs over, the one named last changes fastest.
Arguments:
- sigma: bfloat16 [2, 16384, 16384], P(None, 'row', 'col'), may hold values from -6 to 6
- coeffs: bfloat16 [2, 16384, 384], P(None, 'col'), may hold values from -0.046875 to 0.046875
Outputs:
- hamiltonian: bfloat16 [2, 16384, 16384], P(None, 'row', 'col')
- rotated: float32 [2, 384, 384], P(None, 'row', 'col')
The draws below stay inside these ranges and needn't reach their ends.
All inputs are finite; a program needn't handle non-finite values.
Results may differ from the reference program's by a relative error of at most 0.0031.
Values may be sent and summed in bfloat16 or wider, within the bound.
No kernel may reach another device: no remote copies, remote signals or barrier semaphores. Data moves between devices by JAX's collectives and lax.ppermute only.
A program may use at most 64 MiB of HBM per device.

```python
import math
import jax
import jax.numpy as jnp
from jax import lax

N = 16384
M = 384


def levels(own_key, dims, shards, smallest, largest):
    factor_of, own = 1.0, jax.random.fold_in(own_key, 6)
    for axis_at, blocks in shards:
        heights = jnp.exp(jax.random.uniform(jax.random.fold_in(own, axis_at), (blocks,), jnp.float32, smallest / len(shards), largest / len(shards)))
        factor_of = factor_of * jnp.repeat(heights, dims[axis_at] // blocks).reshape([-1 if axis == axis_at else 1 for axis in range(len(dims))])
    return factor_of


def gaussian(stream_key, extent, spread, most, cuts=(), held_as=jnp.bfloat16):
    values = spread * jax.random.normal(stream_key, extent, jnp.float32)
    if cuts:
        values = values * levels(stream_key, extent, cuts, -0.22, 0.18)
    return jnp.clip(values, -most, most).astype(held_as)


def setup_inputs(seed: int = 0) -> dict:
    streams_of = jax.random.split(jax.random.key(seed), 3)
    return {
        "sigma": gaussian(streams_of[0], (2, N, N), 1.0, 6.0, ((1, 16), (2, 32))),
        "coeffs": gaussian(streams_of[1], (2, N, M), N ** -0.5, 0.046875, ((1, 32),)),
    }


def reference(sigma, coeffs):
    block_size = math.gcd(N, 1024)
    block_count = N // block_size
    coeff_re = coeffs[0]
    coeff_im = coeffs[1]

    def one_block(total, index):
        start = (index * block_size).astype(jnp.int32)
        row_strip = lax.dynamic_slice_in_dim(sigma, start, block_size, 1).astype(jnp.float32)
        col_strip = lax.dynamic_slice_in_dim(sigma, start, block_size, 2).astype(jnp.float32)
        herm_re = (0.5 * (row_strip[0] + col_strip[0].T)).astype(jnp.bfloat16)
        herm_im = (0.5 * (row_strip[1] - col_strip[1].T)).astype(jnp.bfloat16)
        prod_re = jnp.dot(herm_re, coeff_re, preferred_element_type=jnp.float32) - jnp.dot(herm_im, coeff_im, preferred_element_type=jnp.float32)
        prod_im = jnp.dot(herm_re, coeff_im, preferred_element_type=jnp.float32) + jnp.dot(herm_im, coeff_re, preferred_element_type=jnp.float32)
        coeff_rows = lax.dynamic_slice_in_dim(coeffs, start, block_size, 1).astype(jnp.float32)
        high = lax.Precision.HIGHEST
        new_re = total[0] + jnp.dot(coeff_rows[0].T, prod_re, precision=high) + jnp.dot(coeff_rows[1].T, prod_im, precision=high)
        new_im = total[1] + jnp.dot(coeff_rows[0].T, prod_im, precision=high) - jnp.dot(coeff_rows[1].T, prod_re, precision=high)
        return jnp.stack([new_re, new_im]), jnp.stack([herm_re, herm_im])

    start_total = jnp.zeros((2, M, M), jnp.float32)
    rotated, pieces = lax.scan(one_block, start_total, jnp.arange(block_count, dtype=jnp.int32))
    hamiltonian = jnp.transpose(pieces, (1, 0, 2, 3)).reshape(2, N, N)
    return hamiltonian, rotated
```

```python
import jax
import jax.numpy as jnp
from jax import lax
from jax.experimental import pallas as pl
from jax.experimental.pallas import tpu as pltpu
from jax.sharding import PartitionSpec as P

BF16 = jnp.bfloat16
F32 = jnp.float32


def contract(left, right, dims):
    return lax.dot_general(left, right, (dims, ((), ())), preferred_element_type=F32)


def apply(left, right):
    return contract(left, right, ((1,), (0,)))


def apply_left_transposed(left, pieces):
    total = contract(left, pieces[0], ((0,), (0,)))
    for piece in pieces[1:]:
        total = total + contract(left, piece, ((0,), (0,)))
    return total


def split_exact(value):
    high = value.astype(BF16)
    rest = value - high.astype(F32)
    middle = rest.astype(BF16)
    low = (rest - middle.astype(F32)).astype(BF16)
    return high, middle, low


def rotate_kernel(which_ref, strip_ref, own_ref, other_ref, left_ref, out_ref):
    mine = which_ref[0]
    rows = strip_ref.shape[0] * strip_ref.shape[3]
    width = strip_ref.shape[4]

    def tile(side, part):
        return strip_ref[:, side, part].reshape(rows, width)

    own_re, own_im = tile(mine, 0), tile(mine, 1)
    prod_re = apply(own_re, own_ref[0]) - apply(own_im, own_ref[1])
    prod_im = apply(own_re, own_ref[1]) + apply(own_im, own_ref[0])
    far_re, far_im = tile(1 - mine, 0), tile(1 - mine, 1)
    prod_re += apply(far_re, other_ref[0]) - apply(far_im, other_ref[1])
    prod_im += apply(far_re, other_ref[1]) + apply(far_im, other_ref[0])
    states = left_ref.shape[3]
    left_re = left_ref[:, 0].reshape(rows, states)
    left_im = left_ref[:, 1].reshape(rows, states)
    pieces_re, pieces_im = split_exact(prod_re), split_exact(prod_im)
    rot_re = apply_left_transposed(left_re, pieces_re) + apply_left_transposed(left_im, pieces_im)
    rot_im = apply_left_transposed(left_re, pieces_im) - apply_left_transposed(left_im, pieces_re)
    out_ref[0] = 0.5 * (rot_re + rot_re.T)
    out_ref[1] = 0.5 * (rot_im - rot_im.T)


def rotate(which, strip, own, other, left):
    states = own.shape[2]
    vmem = pl.BlockSpec(memory_space=pltpu.VMEM)
    return pl.pallas_call(
        rotate_kernel,
        out_shape=jax.ShapeDtypeStruct((2, states, states), F32),
        in_specs=[pl.BlockSpec(memory_space=pltpu.SMEM), vmem, vmem, vmem, vmem],
        out_specs=vmem,
        compiler_params=pltpu.CompilerParams(vmem_limit_bytes=40 * 1024 * 1024),
        cost_estimate=pl.CostEstimate(flops=4 * 10**9, bytes_accessed=6 * 10**6, transcendentals=0),
    )(which, strip, own, other, left)


def hermitize_kernel(own_ref, mirror_ref, out_ref):
    size = own_ref.shape[2]
    mirror = mirror_ref[...].reshape(size, size).astype(F32).T
    own = own_ref[0].astype(F32)
    sign = jnp.where(pl.program_id(0) == 0, 1.0, -1.0).astype(F32)
    out_ref[0] = (0.5 * (own + sign * mirror)).astype(BF16)


def hermitize(sigma, mirror):
    _, height, width = sigma.shape
    strips, factor, _, strip_rows, _ = mirror.shape
    tile = pl.BlockSpec((1, width, width), lambda part, half: (part, half, 0))
    return pl.pallas_call(
        hermitize_kernel,
        grid=(2, factor),
        out_shape=jax.ShapeDtypeStruct(sigma.shape, BF16),
        in_specs=[
            tile,
            pl.BlockSpec((strips, 1, 1, strip_rows, width), lambda part, half: (0, half, part, 0, 0)),
        ],
        out_specs=tile,
        compiler_params=pltpu.CompilerParams(vmem_limit_bytes=32 * 1024 * 1024),
        cost_estimate=pl.CostEstimate(flops=4 * 10**6, bytes_accessed=6 * 10**6, transcendentals=0),
    )(sigma, mirror)


def exchange(value, dim, bit, axis, count, stride):
    partners = [(i, i ^ stride) for i in range(count)]
    kept = lax.dynamic_index_in_dim(value, bit, dim, keepdims=False)
    given = lax.dynamic_index_in_dim(value, 1 - bit, dim, keepdims=False)
    return kept, lax.ppermute(given, axis, partners)


def halve(value, dim, bit, axis, count, stride):
    kept, got = exchange(value, dim, bit, axis, count, stride)
    return kept + got


def body(sigma, coeffs):
    row_count = lax.axis_size("row")
    col_count = lax.axis_size("col")
    states = coeffs.shape[2]
    factor = col_count // row_count
    depth = col_count // factor
    _, tile_height, tile_width = sigma.shape
    strip_rows = tile_width // row_count
    row = lax.axis_index("row")
    col = lax.axis_index("col")
    side = col % factor

    plane = [
        [r * col_count + factor * z + low for r in range(row_count) for low in range(factor)]
        for z in range(depth)
    ]
    along_z = [[factor * z + low for z in range(depth)] for low in range(factor)]
    swap = [(c, c ^ 1) for c in range(col_count)]

    own_rows = lax.dynamic_slice_in_dim(coeffs, row * strip_rows, strip_rows, 1)
    left = lax.all_gather(own_rows, "col", axis=0, tiled=True, axis_index_groups=along_z)
    left = left.reshape(depth, 2, strip_rows, states)
    other = lax.ppermute(coeffs, "col", swap)

    moving = sigma.reshape(2, factor, row_count, strip_rows, tile_width).transpose(2, 1, 0, 3, 4)
    moving = moving.reshape(row_count * factor, 2, strip_rows, tile_width)
    moving = lax.all_to_all(moving, ("row", "col"), 0, 0, tiled=True, axis_index_groups=plane)
    moving, left = lax.optimization_barrier((moving, left))
    strip = moving.reshape(row_count, factor, 2, strip_rows, tile_width)

    moving = lax.all_to_all(strip, "col", 0, 0, tiled=True, axis_index_groups=along_z)

    term = rotate(side.astype(jnp.int32).reshape(1), strip, coeffs, other, left)
    rest = states // row_count
    core = row % 2
    bits = (row // 8, (row // 4) % 2, (row // 2) % 2)
    part_sum = halve(term.reshape(2, row_count // 2, 2, rest, states), 2, core, "row", row_count, 1)
    part_sum = halve(part_sum, 0, side, "col", col_count, 1)
    part_sum = part_sum.reshape(2, row_count // 4, rest, states)
    part_sum = halve(part_sum, 0, bits[0], "row", row_count, 8)
    part_sum = part_sum.reshape(2, row_count // 8, rest, states)
    part_sum = halve(part_sum, 0, bits[1], "row", row_count, 4)
    part_sum = halve(part_sum, 0, bits[2], "row", row_count, 2)
    part_sum = part_sum.T
    level = depth // 2
    while level:
        part_sum = part_sum.reshape(2, part_sum.shape[0] // 2, rest)
        part_sum = halve(part_sum, 0, (col // (factor * level)) % 2, "col", col_count, factor * level)
        if level == depth // 2:
            moving, part_sum = lax.optimization_barrier((moving, part_sum))
        level //= 2
    part_sum = part_sum.reshape(factor, states // col_count, rest)
    mine, got = exchange(part_sum, 0, side, "col", col_count, 1)
    real = jnp.where(side == 0, mine, got)
    imag = jnp.where(side == 0, got, mine)
    rotated = jnp.stack([real.T, imag.T])

    mirror = lax.all_to_all(moving, "row", 0, 0, tiled=True)
    hamiltonian = hermitize(sigma, mirror)
    return (hamiltonian, rotated)


def solution(mesh):
    in_specs = (P(None, "row", "col"), P(None, "col", None))
    out_specs = (P(None, "row", "col"), P(None, "row", "col"))
    return jax.shard_map(body, mesh=mesh, in_specs=in_specs, out_specs=out_specs, check_vma=False)
```

```python
import jax
import jax.numpy as jnp
from jax import lax
from jax.experimental import pallas as pl
from jax.experimental.pallas import tpu as pltpu
from jax.sharding import PartitionSpec as P

BF16 = jnp.bfloat16
F32 = jnp.float32
ORDER = (0, 4, 2, 6, 1, 5, 3, 7)
STRIDE = 5


def contract(left, right, dims):
    return lax.dot_general(left, right, (dims, ((), ())), preferred_element_type=F32)


def apply(left, right):
    return contract(left, right, ((1,), (0,)))


def split_exact(value):
    high = value.astype(BF16)
    rest = value - high.astype(F32)
    middle = rest.astype(BF16)
    low = (rest - middle.astype(F32)).astype(BF16)
    return high, middle, low


def multiply(strip_ref, side, block_ref):
    rows = strip_ref.shape[0] * strip_ref.shape[3]
    width = strip_ref.shape[4]
    real = strip_ref[:, side, 0].reshape(rows, width)
    imag = strip_ref[:, side, 1].reshape(rows, width)
    prod_re = apply(real, block_ref[0]) - apply(imag, block_ref[1])
    prod_im = apply(real, block_ref[1]) + apply(imag, block_ref[0])
    return prod_re, prod_im


def near_kernel(which_ref, strip_ref, own_ref, out_ref):
    out_ref[0], out_ref[1] = multiply(strip_ref, which_ref[0], own_ref)


def rotate_kernel(which_ref, strip_ref, near_ref, other_ref, left_ref, out_ref):
    prod_re, prod_im = multiply(strip_ref, 1 - which_ref[0], other_ref)
    prod_re += near_ref[0]
    prod_im += near_ref[1]
    rows = near_ref.shape[1]
    states = left_ref.shape[3]
    left = jnp.concatenate(
        [left_ref[:, 0].reshape(rows, states).T, left_ref[:, 1].reshape(rows, states).T], axis=1
    )
    rot_re = rot_im = None
    for real, imag in zip(split_exact(prod_re), split_exact(prod_im)):
        add_re = apply(left, jnp.concatenate([real, imag], axis=0))
        add_im = apply(left, jnp.concatenate([imag, -real], axis=0))
        rot_re = add_re if rot_re is None else rot_re + add_re
        rot_im = add_im if rot_im is None else rot_im + add_im
    rot_re = 0.5 * (rot_re + rot_re.T)
    rot_im = 0.5 * (rot_im - rot_im.T)
    blocks, _, height, _ = out_ref.shape
    for block in range(blocks):
        out_ref[block, 0] = rot_re[block * height : (block + 1) * height]
        out_ref[block, 1] = rot_im[block * height : (block + 1) * height]


def rotate(which, strip, own, other, left, blocks):
    states = own.shape[2]
    rows = strip.shape[0] * strip.shape[3]
    vmem = pl.BlockSpec(memory_space=pltpu.VMEM)
    params = pltpu.CompilerParams(vmem_limit_bytes=40 * 1024 * 1024)
    near = pl.pallas_call(
        near_kernel,
        out_shape=jax.ShapeDtypeStruct((2, rows, states), F32),
        in_specs=[pl.BlockSpec(memory_space=pltpu.SMEM), vmem, vmem],
        out_specs=vmem,
        compiler_params=params,
        cost_estimate=pl.CostEstimate(flops=10**9, bytes_accessed=4 * 10**6, transcendentals=0),
    )(which, strip, own)
    return pl.pallas_call(
        rotate_kernel,
        out_shape=jax.ShapeDtypeStruct((blocks, 2, states // blocks, states), F32),
        in_specs=[pl.BlockSpec(memory_space=pltpu.SMEM), vmem, vmem, vmem, vmem],
        out_specs=vmem,
        compiler_params=params,
        cost_estimate=pl.CostEstimate(flops=3 * 10**9, bytes_accessed=6 * 10**6, transcendentals=0),
    )(which, strip, near, other, left)


def turn_kernel(value_ref, out_ref):
    rows = value_ref.shape[0]
    blocks = out_ref.shape[0]
    width = value_ref.shape[1] // (2 * blocks)
    turned = value_ref[...].T
    for index in range(2 * blocks):
        half = (index % 2) * rows
        out_ref[index // 2, 0:width, half : half + rows] = turned[index * width : (index + 1) * width]


def turn_columns(value, blocks):
    vmem = pl.BlockSpec(memory_space=pltpu.VMEM)
    return pl.pallas_call(
        turn_kernel,
        out_shape=jax.ShapeDtypeStruct((blocks, value.shape[1] // (2 * blocks), 2 * value.shape[0]), F32),
        in_specs=[vmem],
        out_specs=vmem,
    )(value)


def hermitize_kernel(place_ref, own_ref, *refs):
    pieces, out_ref, mirror_ref = refs[:-2], refs[-2], refs[-1]
    size = own_ref.shape[2]
    height = pieces[0].shape[2]
    for index, piece in enumerate(pieces):
        at = pl.multiple_of(place_ref[index] * height, height)
        mirror_ref[pl.ds(at, height), :] = piece[0, 0]
    step = 256
    diagonal = lax.broadcasted_iota(jnp.int32, (step, step), 0) == lax.broadcasted_iota(
        jnp.int32, (step, step), 1
    )
    identity = jnp.where(diagonal, 1.0, 0.0).astype(BF16)
    sign = jnp.where(pl.program_id(0) == 0, 1.0, -1.0).astype(F32)
    for down in range(0, size, step):
        for across in range(0, size, step):
            tile = mirror_ref[across : across + step, down : down + step]
            turned = contract(identity, tile, ((1,), (1,)))
            own = own_ref[0, down : down + step, across : across + step].astype(F32)
            out_ref[0, down : down + step, across : across + step] = (0.5 * (own + sign * turned)).astype(BF16)


def hermitize(place, sigma, pieces):
    _, _, width = sigma.shape
    factor, _, height, _ = pieces[0].shape
    tile = pl.BlockSpec((1, width, width), lambda part, half: (part, half, 0))
    piece = pl.BlockSpec((1, 1, height, width), lambda part, half: (half, part, 0, 0))
    return pl.pallas_call(
        hermitize_kernel,
        grid=(2, factor),
        out_shape=jax.ShapeDtypeStruct(sigma.shape, BF16),
        in_specs=[pl.BlockSpec(memory_space=pltpu.SMEM), tile] + [piece] * len(pieces),
        out_specs=tile,
        scratch_shapes=[pltpu.VMEM((width, width), BF16)],
        compiler_params=pltpu.CompilerParams(vmem_limit_bytes=32 * 1024 * 1024),
        cost_estimate=pl.CostEstimate(flops=10**9, bytes_accessed=6 * 10**6, transcendentals=0),
    )(place, sigma, *pieces)


def body(sigma, coeffs):
    row_count = lax.axis_size("row")
    col_count = lax.axis_size("col")
    states = coeffs.shape[2]
    factor = col_count // row_count
    depth = col_count // factor
    spread = row_count // 2
    _, tile_height, tile_width = sigma.shape
    strip_rows = tile_width // spread
    shard_rows = tile_width // row_count
    row = lax.axis_index("row")
    col = lax.axis_index("col")
    side = col % factor
    both = ("row", "col")

    def device(r, z, low):
        return r * col_count + factor * z + low

    everyone = [(r, z, low) for r in range(row_count) for z in range(depth) for low in range(factor)]
    plane = [
        [device(2 * m + core, z, low) for m in range(spread) for low in range(factor)]
        for core in range(2)
        for z in range(depth)
    ]
    along_z = [[factor * z + low for z in range(depth)] for low in range(factor)]
    swap = [(c, c ^ 1) for c in range(col_count)]

    turn = [
        (device(r, z, low), device(r - r % 2 + z % 2, z - z % 2 + r % 2, low)) for r, z, low in everyone
    ]
    left = lax.dynamic_slice_in_dim(coeffs, row * shard_rows, shard_rows, 1)
    left = lax.ppermute(left, both, turn)
    other = lax.ppermute(coeffs, "col", swap)

    moving = sigma.reshape(2, factor, spread, strip_rows, tile_width).transpose(2, 1, 0, 3, 4)
    moving = moving.reshape(spread * factor, 2, strip_rows, tile_width)
    moving, left = lax.optimization_barrier((moving, left))
    moving = lax.all_to_all(moving, both, 0, 0, tiled=True, axis_index_groups=plane)
    left = lax.all_gather(left, "col", axis=0, tiled=True, axis_index_groups=along_z)
    moving, left = lax.optimization_barrier((moving, left))
    left = left.reshape(depth, 2, shard_rows, states)
    strip = moving.reshape(spread, factor, 2, strip_rows, tile_width)

    first_strip = strip
    strip = lax.optimization_barrier(strip)
    chosen = []
    routes = []
    places = []
    for offset in ORDER:

        def target(r, z):
            return (r // 2 + STRIDE * z + offset) % spread

        route = [
            (device(r, z, low), device(z, 2 * target(r, z) + r % 2, low)) for r, z, low in everyone
        ]
        source = strip if chosen else first_strip
        chosen.append(lax.dynamic_index_in_dim(source, target(row, col // factor), 0, keepdims=False))
        routes.append(route)
        places.append((col // (2 * factor) - STRIDE * row - offset) % spread)

    term = rotate(side.astype(jnp.int32).reshape(1), strip, coeffs, other, left, row_count)
    term = lax.all_to_all(term, "row", 0, 0, tiled=True).sum(0)
    height, length = states // row_count, states // col_count
    term = turn_columns(term.reshape(2 * height, states), col_count)
    chosen[-1], term = lax.optimization_barrier((chosen[-1], term))
    pieces = [lax.ppermute(value, both, route) for value, route in zip(chosen, routes)]
    term = lax.all_to_all(term, "col", 0, 0, tiled=True)

    term = term.sum(0)
    term = jnp.concatenate([term[:, : 2 * height], term[:, 2 * height : 4 * height]], axis=0)
    rotated = term.T.reshape(2, height, length)

    hamiltonian = hermitize(jnp.stack(places).astype(jnp.int32), sigma, pieces)
    return (hamiltonian, rotated)


def solution(mesh):
    in_specs = (P(None, "row", "col"), P(None, "col", None))
    out_specs = (P(None, "row", "col"), P(None, "row", "col"))
    return jax.shard_map(body, mesh=mesh, in_specs=in_specs, out_specs=out_specs, check_vma=False)
```

```python
import jax
import jax.numpy as jnp
from jax import lax
from jax.experimental import pallas as pl
from jax.experimental.pallas import tpu as pltpu
from jax.sharding import PartitionSpec as P

BF16 = jnp.bfloat16
F32 = jnp.float32
ORDER = (0, 4, 2, 6, 1, 5, 3, 7)
STRIDE = 5


def contract(left, right, dims):
    return lax.dot_general(left, right, (dims, ((), ())), preferred_element_type=F32)


def apply(left, right):
    return contract(left, right, ((1,), (0,)))


def split_exact(value):
    high = value.astype(BF16)
    rest = value - high.astype(F32)
    middle = rest.astype(BF16)
    low = (rest - middle.astype(F32)).astype(BF16)
    return high, middle, low


def multiply(strip_ref, side, block_ref):
    rows = strip_ref.shape[0] * strip_ref.shape[3]
    width = strip_ref.shape[4]
    real = strip_ref[:, side, 0].reshape(rows, width)
    imag = strip_ref[:, side, 1].reshape(rows, width)
    prod_re = apply(real, block_ref[0]) - apply(imag, block_ref[1])
    prod_im = apply(real, block_ref[1]) + apply(imag, block_ref[0])
    return prod_re, prod_im


def near_kernel(which_ref, strip_ref, own_ref, out_ref):
    out_ref[0], out_ref[1] = multiply(strip_ref, which_ref[0], own_ref)


def rotate_kernel(which_ref, strip_ref, near_ref, other_ref, left_ref, out_ref):
    prod_re, prod_im = multiply(strip_ref, 1 - which_ref[0], other_ref)
    prod_re += near_ref[0]
    prod_im += near_ref[1]
    rows = near_ref.shape[1]
    states = left_ref.shape[3]
    left = jnp.concatenate(
        [left_ref[:, 0].reshape(rows, states).T, left_ref[:, 1].reshape(rows, states).T], axis=1
    )
    rot_re = rot_im = None
    for real, imag in zip(split_exact(prod_re), split_exact(prod_im)):
        add_re = apply(left, jnp.concatenate([real, imag], axis=0))
        add_im = apply(left, jnp.concatenate([imag, -real], axis=0))
        rot_re = add_re if rot_re is None else rot_re + add_re
        rot_im = add_im if rot_im is None else rot_im + add_im
    rot_re = 0.5 * (rot_re + rot_re.T)
    rot_im = 0.5 * (rot_im - rot_im.T)
    blocks, _, height, _ = out_ref.shape
    for block in range(blocks):
        out_ref[block, 0] = rot_re[block * height : (block + 1) * height]
        out_ref[block, 1] = rot_im[block * height : (block + 1) * height]


def rotate(which, strip, own, other, left, blocks):
    states = own.shape[2]
    rows = strip.shape[0] * strip.shape[3]
    vmem = pl.BlockSpec(memory_space=pltpu.VMEM)
    params = pltpu.CompilerParams(vmem_limit_bytes=40 * 1024 * 1024)
    near = pl.pallas_call(
        near_kernel,
        out_shape=jax.ShapeDtypeStruct((2, rows, states), F32),
        in_specs=[pl.BlockSpec(memory_space=pltpu.SMEM), vmem, vmem],
        out_specs=vmem,
        compiler_params=params,
        cost_estimate=pl.CostEstimate(flops=10**9, bytes_accessed=4 * 10**6, transcendentals=0),
    )(which, strip, own)
    return pl.pallas_call(
        rotate_kernel,
        out_shape=jax.ShapeDtypeStruct((blocks, 2, states // blocks, states), F32),
        in_specs=[pl.BlockSpec(memory_space=pltpu.SMEM), vmem, vmem, vmem, vmem],
        out_specs=vmem,
        compiler_params=params,
        cost_estimate=pl.CostEstimate(flops=3 * 10**9, bytes_accessed=6 * 10**6, transcendentals=0),
    )(which, strip, near, other, left)


def turn_kernel(value_ref, out_ref):
    rows = value_ref.shape[0]
    blocks = out_ref.shape[0]
    width = value_ref.shape[1] // (2 * blocks)
    turned = value_ref[...].T
    for index in range(2 * blocks):
        half = (index % 2) * rows
        out_ref[index // 2, 0:width, half : half + rows] = turned[index * width : (index + 1) * width]


def turn_columns(value, blocks):
    vmem = pl.BlockSpec(memory_space=pltpu.VMEM)
    return pl.pallas_call(
        turn_kernel,
        out_shape=jax.ShapeDtypeStruct((blocks, value.shape[1] // (2 * blocks), 2 * value.shape[0]), F32),
        in_specs=[vmem],
        out_specs=vmem,
    )(value)


def hermitize_kernel(place_ref, own_ref, *refs):
    pieces, out_ref, mirror_ref = refs[:-2], refs[-2], refs[-1]
    size = own_ref.shape[2]
    height = pieces[0].shape[2]
    for index, piece in enumerate(pieces):
        at = pl.multiple_of(place_ref[index] * height, height)
        mirror_ref[pl.ds(at, height), :] = piece[0, 0]
    step = 256
    diagonal = lax.broadcasted_iota(jnp.int32, (step, step), 0) == lax.broadcasted_iota(
        jnp.int32, (step, step), 1
    )
    identity = jnp.where(diagonal, 1.0, 0.0).astype(BF16)
    sign = jnp.where(pl.program_id(0) == 0, 1.0, -1.0).astype(F32)
    for down in range(0, size, step):
        for across in range(0, size, step):
            tile = mirror_ref[across : across + step, down : down + step]
            turned = contract(identity, tile, ((1,), (1,)))
            own = own_ref[0, down : down + step, across : across + step].astype(F32)
            out_ref[0, down : down + step, across : across + step] = (0.5 * (own + sign * turned)).astype(BF16)


def hermitize(place, sigma, pieces):
    _, _, width = sigma.shape
    factor, _, height, _ = pieces[0].shape
    tile = pl.BlockSpec((1, width, width), lambda part, half: (part, half, 0))
    piece = pl.BlockSpec((1, 1, height, width), lambda part, half: (half, part, 0, 0))
    return pl.pallas_call(
        hermitize_kernel,
        grid=(2, factor),
        out_shape=jax.ShapeDtypeStruct(sigma.shape, BF16),
        in_specs=[pl.BlockSpec(memory_space=pltpu.SMEM), tile] + [piece] * len(pieces),
        out_specs=tile,
        scratch_shapes=[pltpu.VMEM((width, width), BF16)],
        compiler_params=pltpu.CompilerParams(vmem_limit_bytes=32 * 1024 * 1024),
        cost_estimate=pl.CostEstimate(flops=10**9, bytes_accessed=6 * 10**6, transcendentals=0),
    )(place, sigma, *pieces)


def body(sigma, coeffs):
    row_count = lax.axis_size("row")
    col_count = lax.axis_size("col")
    states = coeffs.shape[2]
    factor = col_count // row_count
    depth = col_count // factor
    spread = row_count // 2
    _, tile_height, tile_width = sigma.shape
    strip_rows = tile_width // spread
    shard_rows = tile_width // row_count
    row = lax.axis_index("row")
    col = lax.axis_index("col")
    side = col % factor
    both = ("row", "col")

    def device(r, z, low):
        return r * col_count + factor * z + low

    everyone = [(r, z, low) for r in range(row_count) for z in range(depth) for low in range(factor)]
    plane = [
        [device(2 * m + core, z, low) for m in range(spread) for low in range(factor)]
        for core in range(2)
        for z in range(depth)
    ]
    along_z = [[factor * z + low for z in range(depth)] for low in range(factor)]
    swap = [(device(r, z, low), device(r ^ (2 * (r % 2)), z, low ^ 1)) for r, z, low in everyone]

    turn = [
        (device(r, z, low), device(r - r % 2 + z % 2, z - z % 2 + r % 2, low)) for r, z, low in everyone
    ]
    left = lax.dynamic_slice_in_dim(coeffs, row * shard_rows, shard_rows, 1)
    left = lax.ppermute(left, both, turn)
    other = lax.ppermute(coeffs, both, swap)

    moving = sigma.reshape(2, factor, spread, strip_rows, tile_width).transpose(2, 1, 0, 3, 4)
    moving = moving.reshape(spread * factor, 2, strip_rows, tile_width)
    moving, left = lax.optimization_barrier((moving, left))
    moving = lax.all_to_all(moving, both, 0, 0, tiled=True, axis_index_groups=plane)
    left = lax.all_gather(left, "col", axis=0, tiled=True, axis_index_groups=along_z)
    moving, left = lax.optimization_barrier((moving, left))
    left = left.reshape(depth, 2, shard_rows, states)
    strip = moving.reshape(spread, factor, 2, strip_rows, tile_width)

    first_strip = strip
    strip = lax.optimization_barrier(strip)
    chosen = []
    routes = []
    places = []
    for offset in ORDER:

        def target(r, z):
            return (r // 2 + STRIDE * z + offset) % spread

        route = [
            (device(r, z, low), device(z, 2 * target(r, z) + r % 2, low)) for r, z, low in everyone
        ]
        source = strip if chosen else first_strip
        chosen.append(lax.dynamic_index_in_dim(source, target(row, col // factor), 0, keepdims=False))
        routes.append(route)
        places.append((col // (2 * factor) - STRIDE * row - offset) % spread)

    term = rotate(side.astype(jnp.int32).reshape(1), strip, coeffs, other, left, row_count)
    term = lax.all_to_all(term, "row", 0, 0, tiled=True).sum(0)
    height, length = states // row_count, states // col_count
    term = turn_columns(term.reshape(2 * height, states), col_count)
    chosen[-1], term = lax.optimization_barrier((chosen[-1], term))
    pieces = [lax.ppermute(value, both, route) for value, route in zip(chosen, routes)]
    term = lax.all_to_all(term, "col", 0, 0, tiled=True)

    term = term.sum(0)
    term = jnp.concatenate([term[:, : 2 * height], term[:, 2 * height : 4 * height]], axis=0)
    rotated = term.T.reshape(2, height, length)

    hamiltonian = hermitize(jnp.stack(places).astype(jnp.int32), sigma, pieces)
    return (hamiltonian, rotated)


def solution(mesh):
    in_specs = (P(None, "row", "col"), P(None, "col", None))
    out_specs = (P(None, "row", "col"), P(None, "row", "col"))
    return jax.shard_map(body, mesh=mesh, in_specs=in_specs, out_specs=out_specs, check_vma=False)
```

```python
import jax
import jax.numpy as jnp
from jax import lax
from jax.experimental import pallas as pl
from jax.experimental.pallas import tpu as pltpu
from jax.sharding import PartitionSpec as P

BF16 = jnp.bfloat16
F32 = jnp.float32
ORDER = (0, 4, 2, 6, 1, 5, 3, 7)
STRIDE = 5


def contract(left, right, dims):
    return lax.dot_general(left, right, (dims, ((), ())), preferred_element_type=F32)


def apply(left, right):
    return contract(left, right, ((1,), (0,)))


def split_exact(value):
    high = value.astype(BF16)
    rest = value - high.astype(F32)
    middle = rest.astype(BF16)
    low = (rest - middle.astype(F32)).astype(BF16)
    return high, middle, low


def multiply(strip_ref, side, block_ref):
    rows = strip_ref.shape[0] * strip_ref.shape[3]
    width = strip_ref.shape[4]
    real = strip_ref[:, side, 0].reshape(rows, width)
    imag = strip_ref[:, side, 1].reshape(rows, width)
    prod_re = apply(real, block_ref[0]) - apply(imag, block_ref[1])
    prod_im = apply(real, block_ref[1]) + apply(imag, block_ref[0])
    return prod_re, prod_im


def near_kernel(which_ref, strip_ref, own_ref, out_ref):
    out_ref[0], out_ref[1] = multiply(strip_ref, which_ref[0], own_ref)


def rotate_kernel(which_ref, strip_ref, near_ref, other_ref, left_ref, out_ref):
    prod_re, prod_im = multiply(strip_ref, 1 - which_ref[0], other_ref)
    prod_re += near_ref[0]
    prod_im += near_ref[1]
    rows = near_ref.shape[1]
    states = left_ref.shape[3]
    left = jnp.concatenate(
        [left_ref[:, 0].reshape(rows, states).T, left_ref[:, 1].reshape(rows, states).T], axis=1
    )
    rot_re = rot_im = None
    for real, imag in zip(split_exact(prod_re), split_exact(prod_im)):
        add_re = apply(left, jnp.concatenate([real, imag], axis=0))
        add_im = apply(left, jnp.concatenate([imag, -real], axis=0))
        rot_re = add_re if rot_re is None else rot_re + add_re
        rot_im = add_im if rot_im is None else rot_im + add_im
    rot_re = 0.5 * (rot_re + rot_re.T)
    rot_im = 0.5 * (rot_im - rot_im.T)
    blocks, _, height, _ = out_ref.shape
    for block in range(blocks):
        out_ref[block, 0] = rot_re[block * height : (block + 1) * height]
        out_ref[block, 1] = rot_im[block * height : (block + 1) * height]


def rotate(which, strip, own, other, left, blocks):
    states = own.shape[2]
    rows = strip.shape[0] * strip.shape[3]
    vmem = pl.BlockSpec(memory_space=pltpu.VMEM)
    params = pltpu.CompilerParams(vmem_limit_bytes=40 * 1024 * 1024)
    near = pl.pallas_call(
        near_kernel,
        out_shape=jax.ShapeDtypeStruct((2, rows, states), F32),
        in_specs=[pl.BlockSpec(memory_space=pltpu.SMEM), vmem, vmem],
        out_specs=vmem,
        compiler_params=params,
        cost_estimate=pl.CostEstimate(flops=10**9, bytes_accessed=4 * 10**6, transcendentals=0),
    )(which, strip, own)
    return pl.pallas_call(
        rotate_kernel,
        out_shape=jax.ShapeDtypeStruct((blocks, 2, states // blocks, states), F32),
        in_specs=[pl.BlockSpec(memory_space=pltpu.SMEM), vmem, vmem, vmem, vmem],
        out_specs=vmem,
        compiler_params=params,
        cost_estimate=pl.CostEstimate(flops=3 * 10**9, bytes_accessed=6 * 10**6, transcendentals=0),
    )(which, strip, near, other, left)


def turn_kernel(value_ref, out_ref):
    rows = value_ref.shape[0]
    blocks = out_ref.shape[0]
    width = value_ref.shape[1] // (2 * blocks)
    turned = value_ref[...].T
    for index in range(2 * blocks):
        half = (index % 2) * rows
        out_ref[index // 2, 0:width, half : half + rows] = turned[index * width : (index + 1) * width]


def turn_columns(value, blocks):
    vmem = pl.BlockSpec(memory_space=pltpu.VMEM)
    return pl.pallas_call(
        turn_kernel,
        out_shape=jax.ShapeDtypeStruct((blocks, value.shape[1] // (2 * blocks), 2 * value.shape[0]), F32),
        in_specs=[vmem],
        out_specs=vmem,
    )(value)


def hermitize_kernel(place_ref, own_ref, *refs):
    pieces, out_ref, mirror_ref = refs[:-2], refs[-2], refs[-1]
    size = own_ref.shape[2]
    height = pieces[0].shape[2]
    for index, piece in enumerate(pieces):
        at = pl.multiple_of(place_ref[index] * height, height)
        mirror_ref[pl.ds(at, height), :] = piece[0, 0]
    step = 256
    diagonal = lax.broadcasted_iota(jnp.int32, (step, step), 0) == lax.broadcasted_iota(
        jnp.int32, (step, step), 1
    )
    identity = jnp.where(diagonal, 1.0, 0.0).astype(BF16)
    sign = jnp.where(pl.program_id(0) == 0, 1.0, -1.0).astype(F32)
    for down in range(0, size, step):
        for across in range(0, size, step):
            tile = mirror_ref[across : across + step, down : down + step]
            turned = contract(identity, tile, ((1,), (1,)))
            own = own_ref[0, down : down + step, across : across + step].astype(F32)
            out_ref[0, down : down + step, across : across + step] = (0.5 * (own + sign * turned)).astype(BF16)


def hermitize(place, sigma, pieces):
    _, _, width = sigma.shape
    factor, _, height, _ = pieces[0].shape
    tile = pl.BlockSpec((1, width, width), lambda part, half: (part, half, 0))
    piece = pl.BlockSpec((1, 1, height, width), lambda part, half: (half, part, 0, 0))
    return pl.pallas_call(
        hermitize_kernel,
        grid=(2, factor),
        out_shape=jax.ShapeDtypeStruct(sigma.shape, BF16),
        in_specs=[pl.BlockSpec(memory_space=pltpu.SMEM), tile] + [piece] * len(pieces),
        out_specs=tile,
        scratch_shapes=[pltpu.VMEM((width, width), BF16)],
        compiler_params=pltpu.CompilerParams(vmem_limit_bytes=32 * 1024 * 1024),
        cost_estimate=pl.CostEstimate(flops=10**9, bytes_accessed=6 * 10**6, transcendentals=0),
    )(place, sigma, *pieces)


def strips_kernel(tile_ref, out_ref, done):
    parts, factor = tile_ref.shape[:2]
    copies = [
        pltpu.make_async_copy(tile_ref.at[part, half], out_ref.at[:, half, part], done.at[part, half])
        for part in range(parts)
        for half in range(factor)
    ]
    for copy in copies:
        copy.start()
    for copy in copies:
        copy.wait()


def strips(tile):
    parts, factor, count, rows, columns = tile.shape
    return pl.pallas_call(
        strips_kernel,
        out_shape=jax.ShapeDtypeStruct((count, factor, parts, rows, columns), BF16),
        in_specs=[pl.BlockSpec(memory_space=pl.ANY)],
        out_specs=pl.BlockSpec(memory_space=pl.ANY),
        scratch_shapes=[pltpu.SemaphoreType.DMA((parts, factor))],
        cost_estimate=pl.CostEstimate(flops=0, bytes_accessed=4 * 10**6, transcendentals=0),
    )(tile)


def body(sigma, coeffs):
    row_count = lax.axis_size("row")
    col_count = lax.axis_size("col")
    states = coeffs.shape[2]
    factor = col_count // row_count
    depth = col_count // factor
    spread = row_count // 2
    _, tile_height, tile_width = sigma.shape
    strip_rows = tile_width // spread
    shard_rows = tile_width // row_count
    row = lax.axis_index("row")
    col = lax.axis_index("col")
    side = col % factor
    both = ("row", "col")

    def device(r, z, low):
        return r * col_count + factor * z + low

    everyone = [(r, z, low) for r in range(row_count) for z in range(depth) for low in range(factor)]
    plane = [
        [device(2 * m + core, z, low) for m in range(spread) for low in range(factor)]
        for core in range(2)
        for z in range(depth)
    ]
    along_z = [[factor * z + low for z in range(depth)] for low in range(factor)]
    swap = [(device(r, z, low), device(r ^ (2 * (r % 2)), z, low ^ 1)) for r, z, low in everyone]

    turn = [
        (device(r, z, low), device(r - r % 2 + z % 2, z - z % 2 + r % 2, low)) for r, z, low in everyone
    ]
    left = lax.dynamic_slice_in_dim(coeffs, row * shard_rows, shard_rows, 1)
    left = lax.ppermute(left, both, turn)
    other = lax.ppermute(coeffs, both, swap)

    moving = strips(sigma.reshape(2, factor, spread, strip_rows, tile_width))
    moving = moving.reshape(spread * factor, 2, strip_rows, tile_width)
    moving, left = lax.optimization_barrier((moving, left))
    moving = lax.all_to_all(moving, both, 0, 0, tiled=True, axis_index_groups=plane)
    left = lax.all_gather(left, "col", axis=0, tiled=True, axis_index_groups=along_z)
    moving, left = lax.optimization_barrier((moving, left))
    left = left.reshape(depth, 2, shard_rows, states)
    strip = moving.reshape(spread, factor, 2, strip_rows, tile_width)

    first_strip = strip
    strip = lax.optimization_barrier(strip)
    chosen = []
    routes = []
    places = []
    for offset in ORDER:

        def target(r, z):
            return (r // 2 + STRIDE * z + offset) % spread

        route = [
            (device(r, z, low), device(z, 2 * target(r, z) + r % 2, low)) for r, z, low in everyone
        ]
        source = strip if chosen else first_strip
        chosen.append(lax.dynamic_index_in_dim(source, target(row, col // factor), 0, keepdims=False))
        routes.append(route)
        places.append((col // (2 * factor) - STRIDE * row - offset) % spread)

    term = rotate(side.astype(jnp.int32).reshape(1), strip, coeffs, other, left, row_count)
    term = lax.all_to_all(term, "row", 0, 0, tiled=True).sum(0)
    height, length = states // row_count, states // col_count
    term = turn_columns(term.reshape(2 * height, states), col_count)
    chosen[-1], term = lax.optimization_barrier((chosen[-1], term))
    pieces = [lax.ppermute(value, both, route) for value, route in zip(chosen, routes)]
    term = lax.all_to_all(term, "col", 0, 0, tiled=True)

    term = term.sum(0)
    term = jnp.concatenate([term[:, : 2 * height], term[:, 2 * height : 4 * height]], axis=0)
    rotated = term.T.reshape(2, height, length)

    hamiltonian = hermitize(jnp.stack(places).astype(jnp.int32), sigma, pieces)
    return (hamiltonian, rotated)


def solution(mesh):
    in_specs = (P(None, "row", "col"), P(None, "col", None))
    out_specs = (P(None, "row", "col"), P(None, "row", "col"))
    return jax.shard_map(body, mesh=mesh, in_specs=in_specs, out_specs=out_specs, check_vma=False)
```
